32 devices in a mesh: col: 2 (over core), dp: 16 (over z, y, x).
Axes of the slice: x: 2, y: 2, z: 4, core: 2. Of those that a mesh axis runs over, the one named last changes fastest.
Arguments:
- acts: bfloat16 [6144, 5120], P('dp', 'col'), may hold values from -6 to 6
- out_grad: bfloat16 [6144, 8192], P('dp', 'col'), may hold values from -6 to 6
- projection: bfloat16 [5120, 256], replicated, may hold values from -0.078125 to 0.078125
- weight: bfloat16 [5120, 8192], P('dp', 'col'), may hold values from -0.078125 to 0.078125
- m_codes: int32 [256, 8192], P('dp', 'col'), may hold values from -127 to 127
- m_exps: int32 [256, 256], P('dp', 'col'), may hold values from -16 to -9
- v_codes: int32 [256, 8192], P('dp', 'col'), may hold values from 1 to 127
- v_exps: int32 [256, 256], P('dp', 'col'), may hold values from -24 to -18
- next_acts: bfloat16 [6144, 5120], P('dp', 'col'), may hold values from -6 to 6
Outputs:
- next_out: bfloat16 [6144, 8192], P('dp', 'col')
- new_weight: bfloat16 [5120, 8192], P('dp', 'col')
- update: float32 [256, 8192], P('dp', 'col')
The draws below stay inside these ranges and needn't reach their ends.
Inputs may be any that keep to these rules, and one draw needn't show every extreme that they name: `v_codes`: second moment mantissas are positive.
All inputs are finite; a program needn't handle non-finite values.
Results may differ from the reference program's by a relative error of at most 0.0051.
Values may be sent and summed in bfloat16 or wider, within the bound.
A program may use at most 128 MiB of HBM per device.

```python
import jax
import jax.numpy as jnp
from jax import lax

D = 5120
F = 8192
R = 256
BLOCK = 32
TOKENS = 6144


def with_ends(values, rng, least, top_value):
    extent = values.shape
    index_at = [jax.random.randint(jax.random.fold_in(rng, axis), (), 0, extent[axis]) for axis in range(len(extent))]
    values = values.at[tuple(index_at)].set(least)
    longest = extent.index(max(extent))
    index_at[longest] = (index_at[longest] + 1) % extent[longest]
    return values.at[tuple(index_at)].set(top_value)


def block_scale(own_key, shape, pieces, low, high):
    def one(axis_at, shards_of):
        heights = jax.random.uniform(jax.random.fold_in(jax.random.fold_in(own_key, 6), axis_at), (shards_of,), jnp.float32, low / len(pieces), high / len(pieces))
        return jnp.repeat(jnp.exp(heights), shape[axis_at] // shards_of).reshape((-1,) + (1,) * (len(shape) - axis_at - 1))

    loudness = one(*pieces[0])
    for cut in pieces[1:]:
        loudness = loudness * one(*cut)
    return loudness


def bell_draw(rng, extent, width, bound, shards=(), kind=jnp.bfloat16):
    factor_of = block_scale(rng, extent, shards, -0.22, 0.18) if shards else 1.0
    entries = jax.random.normal(rng, extent, jnp.float32) * width * factor_of
    return jnp.minimum(jnp.maximum(entries, -bound), bound).astype(kind)


def setup_inputs(seed: int = 0) -> dict:
    splits = jax.random.split(jax.random.key(seed), 10)
    acts = bell_draw(splits[0], (TOKENS, D), 1.0, 6.0, ((0, 16), (1, 2)))
    out_grad = bell_draw(splits[1], (TOKENS, F), 1.0, 6.0, ((0, 16), (1, 2)))
    projection = bell_draw(splits[2], (D, R), D ** -0.5, 0.078125)
    weight = bell_draw(splits[3], (D, F), D ** -0.5, 0.078125, ((0, 16), (1, 2)))
    m_codes = with_ends(jax.random.randint(splits[4], (R, F), -127, 128), jax.random.fold_in(splits[4], 1), -127, 127).astype(jnp.int32)
    m_exps = with_ends(jax.random.randint(splits[5], (R, F // BLOCK), -16, -8), jax.random.fold_in(splits[5], 1), -16, (-8) - 1).astype(jnp.int32)
    v_codes = with_ends(jax.random.randint(splits[6], (R, F), 1, 128), jax.random.fold_in(splits[6], 1), 1, 127).astype(jnp.int32)
    v_exps = with_ends(jax.random.randint(splits[7], (R, F // BLOCK), -24, -17), jax.random.fold_in(splits[7], 1), -24, (-17) - 1).astype(jnp.int32)
    next_acts = bell_draw(splits[8], (TOKENS, D), 1.0, 6.0, ((0, 16), (1, 2)))
    return {"acts": acts, "out_grad": out_grad, "projection": projection, "weight": weight, "m_codes": m_codes, "m_exps": m_exps, "v_codes": v_codes, "v_exps": v_exps, "next_acts": next_acts}


learn_rate = 0.02
beta_one = 0.9
beta_two = 0.999
epsilon = 1e-08
correct_first = 0.9999734386011124
correct_second = 0.0952078528862904

def decode(codes, exps):
    scale = jnp.exp2(exps.astype(jnp.float32))
    rows = codes.shape[0]
    values = (codes.astype(jnp.float32) / 128.0).reshape(rows, exps.shape[1], codes.shape[1] // exps.shape[1])
    return (values * scale[:, :, None]).reshape(rows, codes.shape[1])

def reference(acts, out_grad, projection, weight, m_codes, m_exps, v_codes, v_exps, next_acts):
    lowrank = jnp.dot(acts, projection, preferred_element_type=jnp.float32).astype(jnp.bfloat16)
    grad = lax.dot_general(lowrank, out_grad, (((0,), (0,)), ((), ())), preferred_element_type=jnp.float32) / TOKENS
    m_old = decode(m_codes, m_exps)
    v_old = decode(v_codes, v_exps)
    first = beta_one * m_old + (1.0 - beta_one) * grad
    second = beta_two * v_old + (1.0 - beta_two) * grad * grad
    update = first / correct_first / (jnp.sqrt(second / correct_second) + epsilon)
    direction = update.astype(jnp.bfloat16)
    delta = jnp.dot(projection, direction, preferred_element_type=jnp.float32)
    new_weight = (weight.astype(jnp.float32) - learn_rate * delta).astype(jnp.bfloat16)
    next_out = jnp.dot(next_acts, new_weight, preferred_element_type=jnp.float32).astype(jnp.bfloat16)
    return (next_out, new_weight, update)
```

```python
import functools

import jax
import jax.numpy as jnp
from jax import lax
from jax.experimental import pallas as pl
from jax.experimental.pallas import tpu as pltpu
from jax.sharding import PartitionSpec as P

learn_rate = 0.02
beta_one = 0.9
beta_two = 0.999
epsilon = 1e-08
correct_first = 0.9999734386011124
correct_second = 0.0952078528862904
MESH = pl.DeviceIdType.MESH
SIDE = 4
SPLITS = 4
BF = jnp.bfloat16
F32 = jnp.float32


def dot(a, b):
    return jnp.dot(a, b, preferred_element_type=F32)


def kernel(
    layers, tokens_all,
    acts, grads, proj, weight, mc, me, vc, ve, nxt,
    out, new_weight, update,
    acts_v, proj_v, grads_v, weight_v, mc_v, me_v, vc_v, ve_v,
    low_v, low_t, gpart, grecv, gz, gsum, dirs, upd_v, nw_v,
    a_v, b_v, n_v, c_v,
    load_sem, low_send, low_recv, g_send, g_recv, gz_send, gz_recv,
    dz_send, dz_recv, di_send, di_recv, a_send, a_fwd, a_recv,
    bi_send, bz_send, b_recv, c_send, c_recv, c_loc, out_sem,
):
    c = lax.axis_index("col")
    dp = lax.axis_index("dp")
    z = dp // SIDE
    q = dp % SIDE
    rows, width = weight.shape
    block = width // SIDE
    part = block // SPLITS
    tok, half = nxt.shape
    rank = proj.shape[1]
    rstep = mc.shape[0]

    def peer(j):
        return ((q // 2 + j // 2) % 2) * 2 + (q % 2 + j % 2) % 2

    def at(zz, qq):
        return (c, zz * SIDE + qq)

    def remote(src, dst, ss, rs, dev):
        return pltpu.make_async_remote_copy(
            src_ref=src, dst_ref=dst, send_sem=ss, recv_sem=rs,
            device_id=dev, device_id_type=MESH,
        )

    other = (1 - c, dp)

    def loop(n, body, first=0):
        def step(i, carry):
            body(i)
            return carry
        lax.fori_loop(first, n, step, 0)

    loads = [
        (acts, acts_v), (proj, proj_v), (grads, grads_v), (weight, weight_v),
        (mc, mc_v), (me, me_v), (vc, vc_v), (ve, ve_v), (nxt, a_v.at[q, c]),
    ]
    loads = [pltpu.make_async_copy(s, d, load_sem.at[i]) for i, (s, d) in enumerate(loads)]
    for copy in loads:
        copy.start()

    barrier = pltpu.get_barrier_semaphore()
    partners = [other] + [at(z, peer(j)) for j in range(1, SIDE)]
    partners += [at((z + o) % layers, q) for o in range(1, layers)]
    for dev in partners:
        pl.semaphore_signal(barrier, inc=1, device_id=dev, device_id_type=MESH)
    pl.semaphore_wait(barrier, len(partners))

    def cols(qq, s):
        return pl.ds(pl.multiple_of(qq * block + s * part, 128), part)

    def b_in(s, j):
        return remote(weight.at[:, cols(peer(j), s)], b_v.at[s, dp],
                      bi_send.at[s, j], b_recv.at[s, dp], at(z, peer(j)))

    def b_own(s):
        return pltpu.make_async_copy(weight.at[:, cols(q, s)], b_v.at[s, dp], bi_send.at[s, 0])

    def b_z(s, dpi, way, own=False):
        src = weight.at[:, cols(q, s)] if own else b_v.at[s, dpi]
        return remote(src, b_v.at[s, dpi], bz_send.at[way, s, dpi], b_recv.at[s, dpi],
                      at((z + (1 if way == 0 else layers - 1)) % layers, q))

    def b_send_z(s, dpi, way, own=False):
        @pl.when((z < layers - 1) if way == 0 else (z > 0))
        def _():
            b_z(s, dpi, way, own).start()

    def b_wait(s, dpi):
        remote(b_v.at[s, dpi], b_v.at[s, dpi], bi_send.at[s, 0], b_recv.at[s, dpi], other).wait_recv()

    def send_in(s):
        for j in range(1, SIDE):
            b_in(s, j).start()
        b_own(s).start()

    def send_own(s):
        for way in range(2):
            b_send_z(s, dp, way, own=True)

    def layer_stage(s):
        def one(j):
            dpi = z * SIDE + peer(j)
            b_wait(s, dpi)
            for way in range(2):
                b_send_z(s, dpi, way)
        loop(SIDE, one, 1)

    def far_stage(s, d):
        def one(j):
            for way in range(2):
                src = z - d if way == 0 else z + d

                @pl.when((src >= 0) & (src < layers))
                def _():
                    dpi = src * SIDE + peer(j)
                    b_wait(s, dpi)
                    b_send_z(s, dpi, way)
        loop(SIDE, one)

    def low_copy():
        return remote(low_v.at[0], low_v.at[1], low_send, low_recv, other)

    def g_copy(j):
        return remote(gpart.at[:, peer(j)], grecv.at[j], g_send.at[j], g_recv.at[j], at(z, peer(j)))

    def gz_copy(o):
        zz = (z + o) % layers
        return remote(gsum.at[zz], gz.at[o], gz_send.at[o], gz_recv.at[o], at(zz, q))

    def dz_copy(o):
        return remote(dirs.at[z, q], dirs.at[z, q], dz_send.at[o], dz_recv.at[o], at((z + o) % layers, q))

    def dz_wait(o):
        zz = (z + layers - o) % layers
        remote(dirs.at[zz, q], dirs.at[zz, q], dz_send.at[o], dz_recv.at[o], other).wait_recv()

    def di_copy(j):
        return remote(dirs.at[:, q], dirs.at[:, q], di_send.at[j], di_recv.at[j], at(z, peer(j)))

    def di_wait(j):
        remote(dirs.at[:, peer(j)], dirs.at[:, peer(j)], di_send.at[j], di_recv.at[j], other).wait_recv()

    def a_copy(j):
        return remote(nxt, a_v.at[q, c], a_send.at[j], a_recv.at[q, c], at(z, peer(j)))

    def a_cross(j):
        qq = peer(j)
        src = nxt if j == 0 else a_v.at[qq, c]
        return remote(src, a_v.at[qq, c], a_fwd.at[j], a_recv.at[qq, c], other)

    def a_wait(qq, cc):
        remote(a_v.at[qq, cc], a_v.at[qq, cc], a_send.at[0], a_recv.at[qq, cc], other).wait_recv()

    wide = 512 if width % 512 == 0 else 128

    def slab(i):
        return pl.ds(pl.multiple_of(i * wide, 128), wide)

    def gradient():
        loads[0].wait()
        loads[1].wait()
        low_v[0] = dot(acts_v[...], proj_v[pl.ds(pl.multiple_of(c * half, 128), half), :])
        low_copy().start()
        loads[2].wait()
        low_copy().wait_recv()
        low_t[...] = jnp.transpose(low_v[0] + low_v[1]).astype(BF)

        def one(i):
            g = dot(low_t[...], grads_v[:, slab(i)])
            gpart[:, :, :, slab(i)] = g.astype(BF).reshape(layers, SIDE, rstep, wide)
        loop(width // wide, one)
        for j in range(1, SIDE):
            g_copy(j).start()

    def gradient_layer():
        for j in range(1, SIDE):
            g_copy(j).wait_recv()

        def one(i):
            total = gpart[:, q, :, slab(i)].astype(F32)
            for j in range(1, SIDE):
                total += grecv[j, :, :, slab(i)].astype(F32)
            gsum[:, :, slab(i)] = total.astype(BF)
        loop(width // wide, one)
        for o in range(1, layers):
            gz_copy(o).start()

    def adam():
        for i in range(4, 8):
            loads[i].wait()
        for o in range(1, layers):
            gz_copy(o).wait_recv()
        blocks = me.shape[1]
        each = width // blocks
        m_scale = jnp.exp2(me_v[...].astype(F32)).astype(BF)
        v_scale = jnp.exp2(ve_v[...].astype(F32)).astype(BF)

        def one(i):
            total = gsum[z, :, slab(i)].astype(F32)
            for o in range(1, layers):
                total += gz[o, :, slab(i)].astype(F32)
            grad = total / tokens_all
            owner = (lax.broadcasted_iota(jnp.int32, (blocks, wide), 1) + i * wide) // each
            pick = (owner == lax.broadcasted_iota(jnp.int32, (blocks, wide), 0)).astype(F32).astype(BF)
            m_old = mc_v[:, slab(i)].astype(F32) / 128.0 * dot(m_scale, pick)
            v_old = vc_v[:, slab(i)].astype(F32) / 128.0 * dot(v_scale, pick)
            first = beta_one * m_old + (1.0 - beta_one) * grad
            second = beta_two * v_old + (1.0 - beta_two) * grad * grad
            u = first / correct_first / (jnp.sqrt(second / correct_second) + epsilon)
            upd_v[:, slab(i)] = u
            dirs[z, q, :, slab(i)] = u.astype(BF)
        loop(width // wide, one)
        for o in range(1, layers):
            dz_copy(o).start()
        pltpu.make_async_copy(upd_v, update, out_sem.at[0]).start()

    def direction_layer():
        for o in range(1, layers):
            dz_wait(o)
        for j in range(1, SIDE):
            di_copy(j).start()

    def weights():
        for j in range(1, SIDE):
            di_wait(j)
        loads[3].wait()

        def one(i):
            d = dirs[:, :, :, slab(i)].reshape(rank, wide)
            delta = dot(proj_v[pl.ds(pl.multiple_of(dp * rows, 16), rows), :], d)
            nw_v[:, slab(i)] = (weight_v[:, slab(i)].astype(F32) - learn_rate * delta).astype(BF)
        loop(width // wide, one)
        pltpu.make_async_copy(nw_v, new_weight, out_sem.at[1]).start()

    def tokens():
        for j in range(1, SIDE):
            a_wait(peer(j), c)
            a_cross(j).start()
        loads[8].wait()
        for j in range(SIDE):
            a_wait(peer(j), 1 - c)

        def one(m):
            n = dot(a_v[m, 0], proj_v[:half, :]) + dot(a_v[m, 1], proj_v[half:, :])
            n_v[m] = (-learn_rate * n).astype(BF)
        loop(SIDE, one)

    def c_copy(s, m):
        return remote(c_v.at[s, m], out.at[:, cols(q, s)], c_send.at[s, m], c_recv.at[s, q], at(z, m))

    def c_local(s):
        return pltpu.make_async_copy(c_v.at[s, q], out.at[:, cols(q, s)], c_loc.at[s])

    per = half // rows

    def product(s):
        b_own(s).wait()

        def one(j):
            m = peer((j + 1) % SIDE)
            d = dirs[:, :, :, cols(q, s)].reshape(rank, part)
            r = dot(n_v[m], d)
            for cc in range(2):
                r += dot(a_v[m, cc], b_v[s, cc * per:(cc + 1) * per].reshape(half, part))
            c_v[s, m] = r.astype(BF)

            @pl.when(m != q)
            def _():
                c_copy(s, m).start()

            @pl.when(m == q)
            def _():
                c_local(s).start()
        loop(SIDE, one)

    send_own(0)
    send_in(0)
    gradient()
    for j in range(1, SIDE):
        a_copy(j).start()
    a_cross(0).start()
    for s in range(1, SPLITS):
        send_in(s)
    extra = [gradient_layer, adam, direction_layer, weights, tokens]
    events = []
    for s in range(SPLITS):
        events.append((layers * s - s - 1.5, s, 0))
        for d in range(1, layers):
            events.append((layers * s - s + d, s, d))
    ready = []
    for _, s, d in sorted(events):
        if d == 0:
            if s:
                send_own(s)
            layer_stage(s)
        else:
            far_stage(s, d)
        if d == layers - 1:
            ready.append(s)
        if extra:
            extra.pop(0)()
        if not extra:
            for t in ready:
                product(t)
            ready = []
    while extra:
        extra.pop(0)()
    for t in ready:
        product(t)

    low_copy().wait_send()
    for j in range(1, SIDE):
        g_copy(j).wait_send()
        di_copy(j).wait_send()
        a_copy(j).wait_send()
    for j in range(SIDE):
        a_cross(j).wait_send()
    for o in range(1, layers):
        gz_copy(o).wait_send()
        dz_copy(o).wait_send()
    for s in range(SPLITS):
        for j in range(1, SIDE):
            b_in(s, j).wait_send()

        def sent(dpi):
            src = dpi // SIDE

            @pl.when((src <= z) & (z < layers - 1))
            def _():
                b_z(s, dpi, 0).wait_send()

            @pl.when((src >= z) & (z > 0))
            def _():
                b_z(s, dpi, 1).wait_send()
        loop(layers * SIDE, sent)
    pltpu.make_async_copy(upd_v, update, out_sem.at[0]).wait()
    pltpu.make_async_copy(nw_v, new_weight, out_sem.at[1]).wait()

    def done(j):
        qq = peer(j)
        for s in range(SPLITS):
            remote(c_v.at[s, 0], out.at[:, cols(qq, s)], c_send.at[s, 0], c_recv.at[s, qq], other).wait_recv()
            c_copy(s, qq).wait_send()
    loop(SIDE, done, 1)
    for s in range(SPLITS):
        c_local(s).wait()


def fused(acts, out_grad, projection, weight, m_codes, m_exps, v_codes, v_exps, next_acts):
    dp = lax.axis_size("dp")
    layers = dp // SIDE
    rows, width = weight.shape
    part = width // SIDE // SPLITS
    tok, half = next_acts.shape
    rank = projection.shape[1]
    rstep = rank // dp
    dma = lambda *s: pltpu.SemaphoreType.DMA(s)
    any_spec = pl.BlockSpec(memory_space=pl.ANY)
    like = lambda x: pltpu.VMEM(x.shape, x.dtype)
    return pl.pallas_call(
        functools.partial(kernel, layers, acts.shape[0] * dp),
        out_shape=(
            jax.ShapeDtypeStruct((tok, width), BF),
            jax.ShapeDtypeStruct((rows, width), BF),
            jax.ShapeDtypeStruct((rstep, width), F32),
        ),
        in_specs=[any_spec] * 9,
        out_specs=(any_spec,) * 3,
        scratch_shapes=[
            like(acts), like(projection), like(out_grad), like(weight),
            like(m_codes), like(m_exps), like(v_codes), like(v_exps),
            pltpu.VMEM((2, acts.shape[0], rank), F32),
            pltpu.VMEM((rank, acts.shape[0]), BF),
            pltpu.VMEM((layers, SIDE, rstep, width), BF),
            pltpu.VMEM((SIDE, layers, rstep, width), BF),
            pltpu.VMEM((layers, rstep, width), BF),
            pltpu.VMEM((layers, rstep, width), BF),
            pltpu.VMEM((layers, SIDE, rstep, width), BF),
            pltpu.VMEM((rstep, width), F32),
            pltpu.VMEM((rows, width), BF),
            pltpu.VMEM((SIDE, 2, tok, half), BF),
            pltpu.VMEM((SPLITS, dp, rows, part), BF),
            pltpu.VMEM((SIDE, tok, rank), BF),
            pltpu.VMEM((SPLITS, SIDE, tok, part), BF),
            dma(9), pltpu.SemaphoreType.DMA, pltpu.SemaphoreType.DMA, dma(SIDE), dma(SIDE),
            dma(layers), dma(layers),
            dma(layers), dma(layers), dma(SIDE), dma(SIDE), dma(SIDE), dma(SIDE), dma(SIDE, 2),
            dma(SPLITS, SIDE), dma(2, SPLITS, dp), dma(SPLITS, dp),
            dma(SPLITS, SIDE), dma(SPLITS, SIDE), dma(SPLITS), dma(2),
        ],
        compiler_params=pltpu.CompilerParams(
            collective_id=0, has_side_effects=True, vmem_limit_bytes=60 * 2**20
        ),
    )(acts, out_grad, projection, weight, m_codes, m_exps, v_codes, v_exps, next_acts)


def decode(codes, exps):
    scale = jnp.exp2(exps.astype(jnp.float32))
    rows = codes.shape[0]
    values = (codes.astype(jnp.float32) / 128.0).reshape(
        rows, exps.shape[1], codes.shape[1] // exps.shape[1]
    )
    return (values * scale[:, :, None]).reshape(rows, codes.shape[1])


def fits(acts, out_grad, projection, weight, m_codes, m_exps, v_codes, v_exps, next_acts):
    dp = lax.axis_size("dp")
    rank = projection.shape[1]
    return (
        lax.axis_size("col") == 2
        and dp % (2 * SIDE) == 0
        and rank % (16 * dp) == 0
        and weight.shape[0] % 16 == 0
        and weight.shape[1] % (SIDE * SPLITS * 128) == 0
        and next_acts.shape[0] % 16 == 0
        and next_acts.shape[1] % 128 == 0
        and acts.shape[0] % 16 == 0
        and next_acts.shape[1] % weight.shape[0] == 0
    )


def body(acts, out_grad, projection, weight, m_codes, m_exps, v_codes, v_exps, next_acts):
    given = (acts, out_grad, projection, weight, m_codes, m_exps, v_codes, v_exps, next_acts)
    if fits(*given):
        return fused(*given)
    col_width = acts.shape[1]
    col_start = lax.axis_index("col") * col_width
    proj_cols = lax.dynamic_slice_in_dim(projection, col_start, col_width, 0)
    partial_value = jnp.dot(acts, proj_cols, preferred_element_type=jnp.float32)
    lowrank = lax.psum(partial_value, "col").astype(jnp.bfloat16)
    tokens_all = acts.shape[0] * lax.axis_size("dp")
    grad = (
        lax.psum_scatter(
            lax.dot_general(
                lowrank, out_grad, (((0,), (0,)), ((), ())), preferred_element_type=jnp.float32
            ),
            "dp",
            scatter_dimension=0,
            tiled=True,
        )
        / tokens_all
    )
    m_old = decode(m_codes, m_exps)
    v_old = decode(v_codes, v_exps)
    first = beta_one * m_old + (1.0 - beta_one) * grad
    second = beta_two * v_old + (1.0 - beta_two) * grad * grad
    update = first / correct_first / (jnp.sqrt(second / correct_second) + epsilon)
    direction = update.astype(jnp.bfloat16)
    full_next = lax.all_gather(next_acts, "col", axis=1, tiled=True)
    row_count = weight.shape[0]
    row_start = lax.axis_index("dp") * row_count
    proj_rows = lax.dynamic_slice_in_dim(projection, row_start, row_count, 0)
    part = proj_rows
    direction_all = lax.all_gather(direction, "dp", axis=0, tiled=True)
    delta = jnp.dot(part, direction_all, preferred_element_type=jnp.float32)
    new_weight = (weight.astype(jnp.float32) - learn_rate * delta).astype(jnp.bfloat16)
    weight_all = lax.all_gather(weight, "dp", axis=0, tiled=True)
    main = jnp.dot(full_next, weight_all, preferred_element_type=jnp.float32)
    low_next = jnp.dot(full_next, projection, preferred_element_type=jnp.float32).astype(
        jnp.bfloat16
    )
    result = main - learn_rate * jnp.dot(
        low_next, direction_all, preferred_element_type=jnp.float32
    )
    return (result.astype(jnp.bfloat16), new_weight, update)


def solution(mesh):
    placed = (
        P("dp", "col"),
        P("dp", "col"),
        P(),
        P("dp", "col"),
        P("dp", "col"),
        P("dp", "col"),
        P("dp", "col"),
        P("dp", "col"),
        P("dp", "col"),
    )
    return jax.shard_map(
        body,
        mesh=mesh,
        in_specs=placed,
        out_specs=(P("dp", "col"), P("dp", "col"), P("dp", "col")),
        check_vma=False,
    )
```

```python
import functools

import jax
import jax.numpy as jnp
from jax import lax
from jax.experimental import pallas as pl
from jax.experimental.pallas import tpu as pltpu
from jax.sharding import PartitionSpec as P

learn_rate = 0.02
beta_one = 0.9
beta_two = 0.999
epsilon = 1e-08
correct_first = 0.9999734386011124
correct_second = 0.0952078528862904
MESH = pl.DeviceIdType.MESH
SIDE = 4
SHARES = (3, 2, 2, 1)
SPLITS = len(SHARES)
UNITS = sum(SHARES)
PLACES = (2, 4, 7, 4, 7, 9, 10)
EARLY = 1
BF = jnp.bfloat16
F32 = jnp.float32


def dot(a, b):
    return jnp.dot(a, b, preferred_element_type=F32)


def kernel(
    layers, tokens_all,
    acts, grads, proj, weight, mc, me, vc, ve, nxt,
    out, new_weight, update,
    acts_v, proj_v, grads_v, weight_v, mc_v, me_v, vc_v, ve_v,
    low_v, low_t, gpart, grecv, gz, gsum, dirs, upd_v, nw_v,
    a_v, b_v, n_v, c_v, acc_v,
    load_sem, low_send, low_recv, g_send, g_recv, gz_send, gz_recv,
    dz_send, dz_recv, di_send, di_recv, a_send, a_fwd, a_recv, ar_send, ar_recv,
    bi_send, bz_send, b_recv, c_send, c_recv, c_loc, out_sem,
):
    c = lax.axis_index("col")
    dp = lax.axis_index("dp")
    z = dp // SIDE
    q = dp % SIDE
    rows, width = weight.shape
    block = width // SIDE
    unit = block // UNITS
    parts = [unit * k for k in SHARES]
    tok, half = nxt.shape
    rank = proj.shape[1]
    rstep = mc.shape[0]

    def peer(j):
        return ((q // 2 + j // 2) % 2) * 2 + (q % 2 + j % 2) % 2

    def at(zz, qq):
        return (c, zz * SIDE + qq)

    def remote(src, dst, ss, rs, dev):
        return pltpu.make_async_remote_copy(
            src_ref=src, dst_ref=dst, send_sem=ss, recv_sem=rs,
            device_id=dev, device_id_type=MESH,
        )

    other = (1 - c, dp)

    def loop(n, body, first=0):
        def step(i, carry):
            body(i)
            return carry
        lax.fori_loop(first, n, step, 0)

    loads = [
        (acts, acts_v), (proj, proj_v), (grads, grads_v), (weight, weight_v),
        (mc, mc_v), (me, me_v), (vc, vc_v), (ve, ve_v), (nxt, a_v.at[q, c]),
    ]
    loads = [pltpu.make_async_copy(s, d, load_sem.at[i]) for i, (s, d) in enumerate(loads)]
    for copy in loads:
        copy.start()

    barrier = pltpu.get_barrier_semaphore()
    partners = [other] + [at(z, peer(j)) for j in range(1, SIDE)]
    partners += [at((z + o) % layers, q) for o in range(1, layers)]
    for dev in partners:
        pl.semaphore_signal(barrier, inc=1, device_id=dev, device_id_type=MESH)
    pl.semaphore_wait(barrier, len(partners))

    def cols(qq, s):
        return pl.ds(pl.multiple_of(qq * block + sum(parts[:s]), 128), parts[s])

    def b_in(s, j):
        return remote(weight.at[:, cols(peer(j), s)], b_v[s].at[dp],
                      bi_send.at[s, j], b_recv.at[s, dp], at(z, peer(j)))

    def b_own(s):
        return pltpu.make_async_copy(weight.at[:, cols(q, s)], b_v[s].at[dp], bi_send.at[s, 0])

    def b_z(s, dpi, way, own=False):
        src = weight.at[:, cols(q, s)] if own else b_v[s].at[dpi]
        return remote(src, b_v[s].at[dpi], bz_send.at[way, s, dpi], b_recv.at[s, dpi],
                      at((z + (1 if way == 0 else layers - 1)) % layers, q))

    def b_send_z(s, dpi, way, own=False):
        @pl.when((z < layers - 1) if way == 0 else (z > 0))
        def _():
            b_z(s, dpi, way, own).start()

    def b_wait(s, dpi):
        remote(b_v[s].at[dpi], b_v[s].at[dpi], bi_send.at[s, 0], b_recv.at[s, dpi], other).wait_recv()

    def send_in(s):
        for j in range(1, SIDE):
            b_in(s, j).start()
        b_own(s).start()

    def send_own(s):
        for way in range(2):
            b_send_z(s, dp, way, own=True)

    def layer_stage(s):
        def one(j):
            dpi = z * SIDE + peer(j)
            b_wait(s, dpi)
            for way in range(2):
                b_send_z(s, dpi, way)
        loop(SIDE, one, 1)

    def far_stage(s, d):
        def one(j):
            for way in range(2):
                src = z - d if way == 0 else z + d

                @pl.when((src >= 0) & (src < layers))
                def _():
                    dpi = src * SIDE + peer(j)
                    b_wait(s, dpi)
                    b_send_z(s, dpi, way)
        loop(SIDE, one)

    def low_copy():
        return remote(low_v.at[0], low_v.at[1], low_send, low_recv, other)

    def g_copy(j):
        return remote(gpart.at[:, peer(j)], grecv.at[j], g_send.at[j], g_recv.at[j], at(z, peer(j)))

    def gz_copy(o):
        zz = (z + o) % layers
        return remote(gsum.at[zz], gz.at[o], gz_send.at[o], gz_recv.at[o], at(zz, q))

    def dz_copy(o):
        return remote(dirs.at[z, q], dirs.at[z, q], dz_send.at[o], dz_recv.at[o], at((z + o) % layers, q))

    def dz_wait(o):
        zz = (z + layers - o) % layers
        remote(dirs.at[zz, q], dirs.at[zz, q], dz_send.at[o], dz_recv.at[o], other).wait_recv()

    def di_copy(j):
        return remote(dirs.at[:, q], dirs.at[:, q], di_send.at[j], di_recv.at[j], at(z, peer(j)))

    def di_wait(j):
        remote(dirs.at[:, peer(j)], dirs.at[:, peer(j)], di_send.at[j], di_recv.at[j], other).wait_recv()

    def a_copy(j):
        return remote(nxt, a_v.at[q, c], a_send.at[j], a_recv.at[q, c], at(z, peer(j)))

    def a_cross(j):
        qq = peer(j)
        src = nxt if j == 0 else a_v.at[qq, c]
        return remote(src, a_v.at[qq, c], a_fwd.at[j], a_recv.at[qq, c], other)

    def a_relay(h):
        span = pl.ds(h * (half // 2), half // 2)
        ref = a_v.at[peer(1 + h), c, :, span]
        return remote(ref, ref, ar_send.at[h], ar_recv.at[h], at(z, peer(2 - h)))

    def a_relay_wait(h):
        span = pl.ds(h * (half // 2), half // 2)
        ref = a_v.at[peer(3), c, :, span]
        remote(ref, ref, ar_send.at[h], ar_recv.at[h], other).wait_recv()

    def a_wait(qq, cc):
        remote(a_v.at[qq, cc], a_v.at[qq, cc], a_send.at[0], a_recv.at[qq, cc], other).wait_recv()

    wide = 512 if width % 512 == 0 else 128

    def slab(i):
        return pl.ds(pl.multiple_of(i * wide, 128), wide)

    def gradient():
        loads[0].wait()
        loads[1].wait()
        low_v[0] = dot(acts_v[...], proj_v[pl.ds(pl.multiple_of(c * half, 128), half), :])
        low_copy().start()
        loads[2].wait()
        low_copy().wait_recv()
        low_t[...] = jnp.transpose(low_v[0] + low_v[1]).astype(BF)

        def one(i):
            g = dot(low_t[...], grads_v[:, slab(i)])
            gpart[:, :, :, slab(i)] = g.astype(BF).reshape(layers, SIDE, rstep, wide)
        loop(width // wide, one)
        for j in range(1, SIDE):
            g_copy(j).start()

    def gradient_layer():
        for j in range(1, SIDE):
            g_copy(j).wait_recv()

        def one(i):
            total = gpart[:, q, :, slab(i)].astype(F32)
            for j in range(1, SIDE):
                total += grecv[j, :, :, slab(i)].astype(F32)
            gsum[:, :, slab(i)] = total.astype(BF)
        loop(width // wide, one)
        for o in range(1, layers):
            gz_copy(o).start()

    def adam():
        for i in range(4, 8):
            loads[i].wait()
        for o in range(1, layers):
            gz_copy(o).wait_recv()
        blocks = me.shape[1]
        each = width // blocks
        m_scale = jnp.exp2(me_v[...].astype(F32)).astype(BF)
        v_scale = jnp.exp2(ve_v[...].astype(F32)).astype(BF)

        def one(i):
            total = gsum[z, :, slab(i)].astype(F32)
            for o in range(1, layers):
                total += gz[o, :, slab(i)].astype(F32)
            grad = total / tokens_all
            owner = (lax.broadcasted_iota(jnp.int32, (blocks, wide), 1) + i * wide) // each
            pick = (owner == lax.broadcasted_iota(jnp.int32, (blocks, wide), 0)).astype(F32).astype(BF)
            m_old = mc_v[:, slab(i)].astype(F32) / 128.0 * dot(m_scale, pick)
            v_old = vc_v[:, slab(i)].astype(F32) / 128.0 * dot(v_scale, pick)
            first = beta_one * m_old + (1.0 - beta_one) * grad
            second = beta_two * v_old + (1.0 - beta_two) * grad * grad
            u = first / correct_first / (jnp.sqrt(second / correct_second) + epsilon)
            upd_v[:, slab(i)] = u
            dirs[z, q, :, slab(i)] = u.astype(BF)
        loop(width // wide, one)
        for o in range(1, layers):
            dz_copy(o).start()
        pltpu.make_async_copy(upd_v, update, out_sem.at[0]).start()

    def direction_layer():
        for o in range(1, layers):
            dz_wait(o)
        for j in range(1, SIDE):
            di_copy(j).start()

    def weights():
        for j in range(1, SIDE):
            di_wait(j)
        loads[3].wait()

        def one(i):
            d = dirs[:, :, :, slab(i)].reshape(rank, wide)
            delta = dot(proj_v[pl.ds(pl.multiple_of(dp * rows, 16), rows), :], d)
            nw_v[:, slab(i)] = (weight_v[:, slab(i)].astype(F32) - learn_rate * delta).astype(BF)
        loop(width // wide, one)
        pltpu.make_async_copy(nw_v, new_weight, out_sem.at[1]).start()

    def relay():
        for h in range(2):
            a_wait(peer(1 + h), c)
            a_relay(h).start()
            a_cross(1 + h).start()

    def cross():
        for h in range(2):
            a_relay_wait(h)
        a_cross(3).start()

    def tokens():
        loads[8].wait()
        for j in range(SIDE):
            a_wait(peer(j), 1 - c)

        def one(m):
            n = dot(a_v[m, 0], proj_v[:half, :]) + dot(a_v[m, 1], proj_v[half:, :])
            n_v[m] = (-learn_rate * n).astype(BF)
        loop(SIDE, one)

    def c_copy(s, m):
        return remote(c_v[s].at[m], out.at[:, cols(q, s)], c_send.at[s, m], c_recv.at[s, q], at(z, m))

    def c_local(s):
        return pltpu.make_async_copy(c_v[s].at[q], out.at[:, cols(q, s)], c_loc.at[s])

    deep = SIDE * rows
    fold = half // deep
    final = jnp.where(z < layers // 2, layers - 1, 0)

    def lay(m, k, s):
        left = a_v[m, k // fold, :, pl.ds(pl.multiple_of((k % fold) * deep, 128), deep)]
        right = b_v[s][pl.ds(k * SIDE, SIDE)].reshape(deep, parts[s])
        return dot(left, right)

    def low(m, s):
        return dot(n_v[m], dirs[:, :, :, cols(q, s)].reshape(rank, parts[s]))

    def leave(s, m, r):
        c_v[s][m] = r.astype(BF)

        @pl.when(m != q)
        def _():
            c_copy(s, m).start()

        @pl.when(m == q)
        def _():
            c_local(s).start()

    def product(s):
        b_own(s).wait()

        def one(j):
            m = peer(SIDE - 1 - j)
            r = low(m, s)
            for k in range(layers):
                r += lay(m, k, s)
            leave(s, m, r)
        loop(SIDE, one)

    def product_start(s):
        b_own(s).wait()

        def one(m):
            r = low(m, s)
            for k in range(1, layers):
                r += lay(m, (final + k) % layers, s)
            acc_v[m] = r
        loop(SIDE, one)

    def product_end(s):
        def one(j):
            m = peer(SIDE - 1 - j)
            leave(s, m, acc_v[m] + lay(m, final, s))
        loop(SIDE, one)

    events = []
    for s in range(SPLITS):
        events.append((layers * s - s - 1.5, s, 0))
        for d in range(1, layers):
            events.append((layers * s - s + d, s, d))
    events.sort()
    last = len(events) - 1

    def spread():
        for j in range(1, 3):
            a_copy(j).start()
        a_cross(0).start()

    steps = [
        (PLACES[0], gradient_layer), (PLACES[1], adam), (PLACES[2], direction_layer),
        (PLACES[3], relay), (PLACES[4], cross), (PLACES[5], weights), (PLACES[6], tokens),
    ]
    places = [(p * last // 15, step) for p, step in steps]
    send_own(0)
    send_in(0)
    if EARLY:
        send_own(1)
    gradient()
    send_in(1)
    spread()
    ready = []
    for i, (_, s, d) in enumerate(events):
        if i == last:
            for t in ready:
                product(t)
            product_start(s)
        if d == 0:
            if s > EARLY:
                send_own(s)
            layer_stage(s)
            if 0 < s < SPLITS - 1:
                send_in(s + 1)
        else:
            far_stage(s, d)
        for p, step in places:
            if p == i:
                step()
        if d == layers - 1 and i < last:
            ready.append(s)
        if i >= places[-1][0] and ready:
            product(ready.pop(0))
    product_end(SPLITS - 1)

    low_copy().wait_send()
    for j in range(1, SIDE):
        g_copy(j).wait_send()
        di_copy(j).wait_send()
    for j in range(2):
        a_copy(1 + j).wait_send()
        a_relay(j).wait_send()
    for j in range(SIDE):
        a_cross(j).wait_send()
    for o in range(1, layers):
        gz_copy(o).wait_send()
        dz_copy(o).wait_send()
    for s in range(SPLITS):
        for j in range(1, SIDE):
            b_in(s, j).wait_send()

        def sent(dpi):
            src = dpi // SIDE

            @pl.when((src <= z) & (z < layers - 1))
            def _():
                b_z(s, dpi, 0).wait_send()

            @pl.when((src >= z) & (z > 0))
            def _():
                b_z(s, dpi, 1).wait_send()
        loop(layers * SIDE, sent)
    pltpu.make_async_copy(upd_v, update, out_sem.at[0]).wait()
    pltpu.make_async_copy(nw_v, new_weight, out_sem.at[1]).wait()

    def done(j):
        qq = peer(j)
        for s in range(SPLITS):
            remote(c_v[s].at[0], out.at[:, cols(qq, s)], c_send.at[s, 0], c_recv.at[s, qq], other).wait_recv()
            c_copy(s, qq).wait_send()
    loop(SIDE, done, 1)
    for s in range(SPLITS):
        c_local(s).wait()


def fused(acts, out_grad, projection, weight, m_codes, m_exps, v_codes, v_exps, next_acts):
    dp = lax.axis_size("dp")
    layers = dp // SIDE
    rows, width = weight.shape
    parts = [width // SIDE // UNITS * k for k in SHARES]
    tok, half = next_acts.shape
    rank = projection.shape[1]
    rstep = rank // dp
    dma = lambda *s: pltpu.SemaphoreType.DMA(s)
    any_spec = pl.BlockSpec(memory_space=pl.ANY)
    like = lambda x: pltpu.VMEM(x.shape, x.dtype)
    return pl.pallas_call(
        functools.partial(kernel, layers, acts.shape[0] * dp),
        out_shape=(
            jax.ShapeDtypeStruct((tok, width), BF),
            jax.ShapeDtypeStruct((rows, width), BF),
            jax.ShapeDtypeStruct((rstep, width), F32),
        ),
        in_specs=[any_spec] * 9,
        out_specs=(any_spec,) * 3,
        scratch_shapes=[
            like(acts), like(projection), like(out_grad), like(weight),
            like(m_codes), like(m_exps), like(v_codes), like(v_exps),
            pltpu.VMEM((2, acts.shape[0], rank), F32),
            pltpu.VMEM((rank, acts.shape[0]), BF),
            pltpu.VMEM((layers, SIDE, rstep, width), BF),
            pltpu.VMEM((SIDE, layers, rstep, width), BF),
            pltpu.VMEM((layers, rstep, width), BF),
            pltpu.VMEM((layers, rstep, width), BF),
            pltpu.VMEM((layers, SIDE, rstep, width), BF),
            pltpu.VMEM((rstep, width), F32),
            pltpu.VMEM((rows, width), BF),
            pltpu.VMEM((SIDE, 2, tok, half), BF),
            [pltpu.VMEM((dp, rows, part), BF) for part in parts],
            pltpu.VMEM((SIDE, tok, rank), BF),
            [pltpu.VMEM((SIDE, tok, part), BF) for part in parts],
            pltpu.VMEM((SIDE, tok, parts[-1]), F32),
            dma(9), pltpu.SemaphoreType.DMA, pltpu.SemaphoreType.DMA, dma(SIDE), dma(SIDE),
            dma(layers), dma(layers),
            dma(layers), dma(layers), dma(SIDE), dma(SIDE), dma(SIDE), dma(SIDE), dma(SIDE, 2), dma(2), dma(2),
            dma(SPLITS, SIDE), dma(2, SPLITS, dp), dma(SPLITS, dp),
            dma(SPLITS, SIDE), dma(SPLITS, SIDE), dma(SPLITS), dma(2),
        ],
        compiler_params=pltpu.CompilerParams(
            collective_id=0, has_side_effects=True, vmem_limit_bytes=60 * 2**20
        ),
    )(acts, out_grad, projection, weight, m_codes, m_exps, v_codes, v_exps, next_acts)


def decode(codes, exps):
    scale = jnp.exp2(exps.astype(jnp.float32))
    rows = codes.shape[0]
    values = (codes.astype(jnp.float32) / 128.0).reshape(
        rows, exps.shape[1], codes.shape[1] // exps.shape[1]
    )
    return (values * scale[:, :, None]).reshape(rows, codes.shape[1])


def fits(acts, out_grad, projection, weight, m_codes, m_exps, v_codes, v_exps, next_acts):
    dp = lax.axis_size("dp")
    rank = projection.shape[1]
    return (
        lax.axis_size("col") == 2
        and dp % (2 * SIDE) == 0
        and rank % (16 * dp) == 0
        and weight.shape[0] % 16 == 0
        and weight.shape[1] % (SIDE * UNITS * 128) == 0
        and next_acts.shape[0] % 16 == 0
        and next_acts.shape[1] % 256 == 0
        and acts.shape[0] % 16 == 0
        and next_acts.shape[1] % (SIDE * weight.shape[0]) == 0
        and SIDE * weight.shape[0] % 128 == 0
    )


def body(acts, out_grad, projection, weight, m_codes, m_exps, v_codes, v_exps, next_acts):
    given = (acts, out_grad, projection, weight, m_codes, m_exps, v_codes, v_exps, next_acts)
    if fits(*given):
        return fused(*given)
    col_width = acts.shape[1]
    col_start = lax.axis_index("col") * col_width
    proj_cols = lax.dynamic_slice_in_dim(projection, col_start, col_width, 0)
    partial_value = jnp.dot(acts, proj_cols, preferred_element_type=jnp.float32)
    lowrank = lax.psum(partial_value, "col").astype(jnp.bfloat16)
    tokens_all = acts.shape[0] * lax.axis_size("dp")
    grad = (
        lax.psum_scatter(
            lax.dot_general(
                lowrank, out_grad, (((0,), (0,)), ((), ())), preferred_element_type=jnp.float32
            ),
            "dp",
            scatter_dimension=0,
            tiled=True,
        )
        / tokens_all
    )
    m_old = decode(m_codes, m_exps)
    v_old = decode(v_codes, v_exps)
    first = beta_one * m_old + (1.0 - beta_one) * grad
    second = beta_two * v_old + (1.0 - beta_two) * grad * grad
    update = first / correct_first / (jnp.sqrt(second / correct_second) + epsilon)
    direction = update.astype(jnp.bfloat16)
    full_next = lax.all_gather(next_acts, "col", axis=1, tiled=True)
    row_count = weight.shape[0]
    row_start = lax.axis_index("dp") * row_count
    proj_rows = lax.dynamic_slice_in_dim(projection, row_start, row_count, 0)
    part = proj_rows
    direction_all = lax.all_gather(direction, "dp", axis=0, tiled=True)
    delta = jnp.dot(part, direction_all, preferred_element_type=jnp.float32)
    new_weight = (weight.astype(jnp.float32) - learn_rate * delta).astype(jnp.bfloat16)
    weight_all = lax.all_gather(weight, "dp", axis=0, tiled=True)
    main = jnp.dot(full_next, weight_all, preferred_element_type=jnp.float32)
    low_next = jnp.dot(full_next, projection, preferred_element_type=jnp.float32).astype(
        jnp.bfloat16
    )
    result = main - learn_rate * jnp.dot(
        low_next, direction_all, preferred_element_type=jnp.float32
    )
    return (result.astype(jnp.bfloat16), new_weight, update)


def solution(mesh):
    placed = (
        P("dp", "col"),
        P("dp", "col"),
        P(),
        P("dp", "col"),
        P("dp", "col"),
        P("dp", "col"),
        P("dp", "col"),
        P("dp", "col"),
        P("dp", "col"),
    )
    return jax.shard_map(
        body,
        mesh=mesh,
        in_specs=placed,
        out_specs=(P("dp", "col"), P("dp", "col"), P("dp", "col")),
        check_vma=False,
    )
```
